32 devices in a mesh: group: 2 (over x), node: 16 (over z, y, core).
Axes of the slice: x: 2, y: 2, z: 4, core: 2. Of those that a mesh axis runs over, the one named last changes fastest.
Arguments:
- tokens: bfloat16 [2048, 3584], P(('group', 'node')), parts along dimension 0, may hold values from -6 to 6
- expert_ids: int32 [2048, 8], P(('group', 'node')), parts along dimension 0, may hold values from 0 to 15, all different within a row; in each aligned block of 64 rows (0 to 63, 64 to 127, ...) at most 40 rows name the same one
- gate_scores: float32 [2048, 8], P(('group', 'node')), parts along dimension 0, may hold values from 0.05 to 1
- w_gate: bfloat16 [3584, 16384], P(None, 'node'), may hold values from -0.09375 to 0.09375
- w_up: bfloat16 [3584, 16384], P(None, 'node'), may hold values from -0.09375 to 0.09375
- w_down: bfloat16 [16384, 3584], P('node'), may hold values from -0.1875 to 0.1875
Outputs:
- combined: bfloat16 [2048, 3584], P(('group', 'node')), parts along dimension 0
The draws below stay inside these ranges and needn't reach their ends.
There are 2 independent parts, one for each index of `group`. The reference program is written for one: setup_inputs(seed, part) draws one part's arguments, and reference() takes and returns one part's arrays. A program takes and returns all parts, laid end to end along the dimension named above; an argument that names none is the same for every part. Nothing has to cross between parts.
Inputs may be any that keep to these rules, and one draw needn't show every extreme that they name: `expert_ids`: each row names 8 different experts. In the 64 rows of one device no expert is named by more than 40 rows, a bound that some block reaches.
All inputs are finite; a program needn't handle non-finite values.
Results may differ from the reference program's by a relative error of at most 0.0058.
Values may be sent and summed in bfloat16 or wider, within the bound.
A program may use at most 128 MiB of HBM per device.

```python
import math
import jax
import jax.numpy as jnp
import numpy as np
from jax import lax

D = 3584
HID = 1024
TOP = 8
TOK_DEV = 64
EXPERTS = 16
SPLIT = 1
CAP = 40
TOKENS = 1024
N_NODE = 16


def levels(stream_key, extent, pieces, least, high):
    def one(axis_at, parts):
        draws = jax.random.uniform(jax.random.fold_in(jax.random.fold_in(stream_key, 6), axis_at), (parts,), jnp.float32, least / len(pieces), high / len(pieces))
        return jnp.repeat(jnp.exp(draws), extent[axis_at] // parts).reshape((-1,) + (1,) * (len(extent) - axis_at - 1))

    level = one(*pieces[0])
    for cut in pieces[1:]:
        level = level * one(*cut)
    return level


def routed_block(own_key, own, number, rows, amount, top, limit, skew):
    order = jax.random.permutation(own_key, amount)
    packed, usual = portions_of(amount, rows * top, limit, skew, True), portions_of(amount, rows * top, limit, skew, False)
    places = jnp.arange(amount)

    def named(sizes, turn):
        used = int((sizes > 0).sum())
        fixed = max(1, used // 4)
        moved = fixed + (places - fixed + turn * (used - fixed)) % max(1, amount - fixed)
        return jnp.zeros((amount,), jnp.int32).at[order[jnp.where(places < fixed, places, moved)]].set(jnp.asarray(sizes, jnp.int32))

    sizes = jnp.where(number % 4 == 0, named(packed, number // 4), named(usual, number - number // 4 - 1))
    mixed = jax.random.permutation(jax.random.fold_in(own, 3), amount)
    giver, receiver = mixed[0:amount // 2 * 2:2], mixed[1:amount // 2 * 2:2]
    margin = jnp.minimum(sizes[giver] - 1, limit - sizes[receiver]) // 2
    margin = jnp.where((giver == order[0]) | (receiver == order[0]) | (sizes[receiver] == 0), 0, jnp.maximum(margin, 0))
    moved = jax.random.randint(jax.random.fold_in(own, 4), (amount // 2,), 0, 1 << 20) % (margin + 1)
    sizes = sizes.at[giver].add(-moved).at[receiver].add(moved)
    labels = jnp.searchsorted(jnp.cumsum(sizes), jnp.arange(rows * top), side="right").astype(jnp.int32)
    grid = labels.reshape(top, rows).T
    grid = grid[jax.random.permutation(jax.random.fold_in(own, 1), rows)]
    turn = jax.random.randint(jax.random.fold_in(own, 2), (rows, 1), 0, top)
    return jnp.take_along_axis(grid, (jnp.arange(top)[None, :] + turn) % top, axis=1)


def portions_of(count, total, most, slope, full):
    weights = [(1 << 20) // math.isqrt(grade ** slope) + 1 for grade in range(1, count + 1)]
    largest = most if full else min(most, max(-(-total // count), total * weights[0] // sum(weights)))
    least = 1 if total - largest >= count - 1 else 0
    given, surplus = [largest] + [least] * (count - 1), total - largest - least * (count - 1)
    while surplus > 0:
        candidates = [i for i in range(1, count) if given[i] < largest] or [i for i in range(1, count) if given[i] < most]
        pool, remaining = sum([weights[i] for i in candidates]), surplus
        for i in candidates:
            more = min(most - given[i], max(1, remaining * weights[i] // pool), surplus)
            given[i] = given[i] + more
            surplus = surplus - more
    return np.array(given)


def gaussian(own_key, dims, scale, limit, pieces=(), kind=jnp.bfloat16):
    level = levels(own_key, dims, pieces, -0.22, 0.18) if pieces else 1.0
    result = jax.random.normal(own_key, dims, jnp.float32) * scale * level
    return jnp.minimum(jnp.maximum(result, -limit), limit).astype(kind)


def setup_inputs(seed: int = 0, part: int = 0) -> dict:
    key_of = jax.random.split(jax.random.key(seed), 7)
    part_splits = jax.random.split(jax.random.fold_in(key_of[6], part), 7)
    tokens = gaussian(part_splits[0], (TOKENS, D), 1.0, 6.0, ((0, 16),))
    expert_ids_keys = jax.random.split(jax.random.fold_in(part_splits[1], 1), TOKENS // TOK_DEV)
    expert_ids_turns = jax.random.permutation(jax.random.fold_in(part_splits[1], 3), TOKENS // TOK_DEV)
    expert_ids = jax.vmap(lambda own, number: routed_block(jax.random.fold_in(part_splits[1], 2), own, number, TOK_DEV, EXPERTS, TOP, CAP, 2))(expert_ids_keys, expert_ids_turns).reshape((TOKENS, TOP))
    gate_scores = jnp.clip(jnp.exp(math.log(1.0) - 2.9957323 * jax.random.uniform(part_splits[2], (TOKENS, TOP), jnp.float32) ** levels(part_splits[2], (TOKENS, TOP), ((0, 16),), -0.2, 0.2)), 0.05, 1.0)
    w_gate = gaussian(key_of[3], (D, EXPERTS * HID), D ** -0.5, 0.09375, ((1, 16),))
    w_up = gaussian(key_of[4], (D, EXPERTS * HID), D ** -0.5, 0.09375, ((1, 16),))
    w_down = gaussian(key_of[5], (EXPERTS * HID, D), HID ** -0.5, 0.1875, ((0, 16),))
    return {"tokens": tokens, "expert_ids": expert_ids, "gate_scores": gate_scores, "w_gate": w_gate, "w_up": w_up, "w_down": w_down}


ROUTE_SCALE = 2.5


def reference(tokens, expert_ids, gate_scores, w_gate, w_up, w_down):
    weights = ROUTE_SCALE * gate_scores / jnp.sum(gate_scores, axis=1, keepdims=True)
    flat_ids = expert_ids.reshape(-1)
    flat_weights = weights.reshape(-1)
    token_of = (jnp.arange(flat_ids.shape[0], dtype=jnp.int32) // TOP).astype(jnp.int32)
    slot_total = N_NODE * CAP
    block = HID // SPLIT

    def accumulate(running, expert_id):
        hit = flat_ids == expert_id
        ranks = (jnp.cumsum(hit.astype(jnp.int32)) - 1).astype(jnp.int32)
        target = jnp.where(hit, ranks, slot_total).astype(jnp.int32)
        buffer_rows = jnp.zeros((slot_total,), jnp.int32).at[target].set(token_of, mode="drop")
        buffer_weights = jnp.zeros((slot_total,), jnp.float32).at[target].set(flat_weights, mode="drop")
        rows = jnp.take(tokens, buffer_rows, axis=0)
        start = (expert_id * HID).astype(jnp.int32)
        gate_cols = lax.dynamic_slice_in_dim(w_gate, start, HID, 1)
        up_cols = lax.dynamic_slice_in_dim(w_up, start, HID, 1)
        down_rows = lax.dynamic_slice_in_dim(w_down, start, HID, 0)
        gate_part = jnp.dot(rows, gate_cols, preferred_element_type=jnp.float32)
        up_part = jnp.dot(rows, up_cols, preferred_element_type=jnp.float32)
        hidden = (jax.nn.silu(gate_part) * up_part).astype(jnp.bfloat16)
        expert_out = jnp.zeros((slot_total, tokens.shape[1]), jnp.float32)
        for piece_index in range(SPLIT):
            piece = jnp.dot(hidden[:, piece_index * block:(piece_index + 1) * block],
                            down_rows[piece_index * block:(piece_index + 1) * block, :],
                            preferred_element_type=jnp.float32).astype(jnp.bfloat16)
            expert_out = expert_out + piece.astype(jnp.float32)
        rounded = lax.optimization_barrier(expert_out.astype(jnp.bfloat16))
        expert_out = rounded.astype(jnp.float32)
        running = running.at[buffer_rows].add(buffer_weights[:, None] * expert_out)
        return running, None

    start_sum = jnp.zeros((tokens.shape[0], tokens.shape[1]), jnp.float32)
    running, _ = lax.scan(accumulate, start_sum, jnp.arange(EXPERTS, dtype=jnp.int32))
    return running.astype(jnp.bfloat16)
```

```python
import jax
import jax.numpy as jnp
from jax import lax
from jax.sharding import PartitionSpec as P

ROUTE_SCALE = 2.5


def shards(tokens, expert_ids, gate_scores, w_gate, w_up, w_down):
    node_count = lax.axis_size("node")
    experts = max(16, node_count // 2)
    slices = node_count // experts
    weights = ROUTE_SCALE * gate_scores / jnp.sum(gate_scores, axis=1, keepdims=True)
    marks = expert_ids[:, :, None] == jnp.arange(experts, dtype=jnp.int32)[None, None, :]
    table = jnp.sum(jnp.where(marks, weights[:, :, None], 0.0), axis=1)
    all_table = lax.all_gather(table, "node", axis=0, tiled=True)
    own = lax.axis_index("node") // slices
    share = lax.dynamic_slice_in_dim(all_table, own, 1, 1)
    rows = lax.all_gather(tokens, "node", axis=0, tiled=True)
    gate_part = jnp.dot(rows, w_gate, preferred_element_type=jnp.float32)
    up_part = jnp.dot(rows, w_up, preferred_element_type=jnp.float32)
    hidden = (jax.nn.silu(gate_part) * up_part).astype(jnp.bfloat16)
    piece = jnp.dot(hidden, w_down, preferred_element_type=jnp.float32)
    part = (piece * share).astype(jnp.bfloat16)
    return lax.psum_scatter(part, "node", scatter_dimension=0, tiled=True)


def solution(mesh):
    return jax.shard_map(
        shards,
        mesh=mesh,
        in_specs=(
            P(("group", "node"), None),
            P(("group", "node"), None),
            P(("group", "node"), None),
            P(None, "node"),
            P(None, "node"),
            P("node", None),
        ),
        out_specs=P(("group", "node"), None),
        check_vma=False,
    )
```

```python
import jax
import jax.numpy as jnp
from jax import lax
from jax.experimental import pallas as pl
from jax.experimental.pallas import tpu as pltpu
from jax.sharding import PartitionSpec as P

ROUTE_SCALE = 2.5
PLANES = 4
TILES = 4
LANES = 128


def routing_table(expert_ids, gate_scores, experts):
    weights = ROUTE_SCALE * gate_scores / jnp.sum(gate_scores, axis=1, keepdims=True)
    marks = expert_ids[:, :, None] == jnp.arange(experts, dtype=jnp.int32)[None, None, :]
    return jnp.sum(jnp.where(marks, weights[:, :, None], 0.0), axis=1)


def kernel(
    tok, wg_hbm, wu_hbm, wd_hbm, out,
    wg, wu, wd, rows, hidden, part, sib, ybuf, zbuf, acc,
    w_sem, gz_s, gz_r, gy_s, gy_r, gc_s, gc_r, sc_s, sc_r, sy_s, sy_r, sz_s, sz_r,
):
    n = tok.shape[0]
    features = wg_hbm.shape[0]
    hid = wg_hbm.shape[1]
    width = features // TILES
    step_cols = 256
    me = lax.axis_index("node")
    z, y, c = me // 4, (me // 2) % 2, me % 2
    top = PLANES - 1
    mine = pl.ds(pl.multiple_of(y * n, n), n)
    theirs = pl.ds(pl.multiple_of((1 - y) * n, n), n)

    def dev(zz, yy, cc):
        return {"node": zz * 4 + yy * 2 + cc}

    def remote(src, dst, s, r, target):
        return pltpu.make_async_remote_copy(
            src_ref=src, dst_ref=dst, send_sem=s, recv_sem=r,
            device_id=target, device_id_type=pl.DeviceIdType.MESH,
        )

    loads = [
        pltpu.make_async_copy(a, b, w_sem.at[i])
        for i, (a, b) in enumerate(((wg_hbm, wg), (wu_hbm, wu), (wd_hbm, wd)))
    ]
    for load in loads:
        load.start()
    rows[z, c, mine, :] = tok[...]

    barrier = pltpu.get_barrier_semaphore()

    def greet(target):
        pl.semaphore_signal(barrier, inc=1, device_id=target, device_id_type=pl.DeviceIdType.MESH)

    greet(dev(z, 1 - y, c))
    greet(dev(z, y, 1 - c))

    @pl.when(z > 0)
    def _():
        greet(dev(z - 1, y, c))

    @pl.when(z < top)
    def _():
        greet(dev(z + 1, y, c))

    pl.semaphore_wait(barrier, jnp.where(jnp.logical_or(z == 0, z == top), 3, 4))

    flip = z // 2
    m = z + flip * (top - 2 * z)

    def plane(digit):
        return digit + flip * (top - 2 * digit)

    second, third = plane(1 + m), plane(2 - 2 * m)
    last = plane(3)

    def order(k):
        return jnp.where(k == 0, z, jnp.where(k == 1, second, jnp.where(k == 2, third, last)))

    def up_copy(p):
        ref = rows.at[p, c, mine, :]
        return remote(ref, ref, gz_s.at[p, 0], gz_r.at[p], dev(z + 1, y, c))

    def down_copy(p):
        ref = rows.at[p, c, mine, :]
        return remote(ref, ref, gz_s.at[p, 1], gz_r.at[p], dev(z - 1, y, c))

    def y_copy(p):
        ref = rows.at[p, c, mine, :]
        return remote(ref, ref, gy_s.at[p], gy_r.at[p], dev(z, 1 - y, c))

    def y_arrival(p):
        ref = rows.at[p, c, theirs, :]
        return remote(ref, ref, gy_s.at[p], gy_r.at[p], dev(z, 1 - y, c))

    def core_copy(p):
        ref = rows.at[p, c]
        return remote(ref, ref, gc_s.at[p], gc_r.at[p], dev(z, y, 1 - c))

    def core_arrival(p):
        ref = rows.at[p, 1 - c]
        return remote(ref, ref, gc_s.at[p], gc_r.at[p], dev(z, y, 1 - c))

    def goes_up(p):
        return jnp.logical_and(p <= z, z < top)

    def goes_down(p):
        return jnp.logical_and(p >= z, z > 0)

    def forward(p):
        @pl.when(p != z)
        def _():
            ref = rows.at[p, c, mine, :]
            remote(ref, ref, gz_s.at[p, 0], gz_r.at[p], dev(z, 1 - y, c)).wait_recv()

        @pl.when(goes_up(p))
        def _():
            up_copy(p).start()

        @pl.when(goes_down(p))
        def _():
            down_copy(p).start()

    def advance(k):
        @pl.when(jnp.logical_and(m == 0, k <= 3))
        def _():
            forward(order(k))

        @pl.when(jnp.logical_and(m == 1, k == 1))
        def _():
            forward(second)
            forward(third)

        @pl.when(jnp.logical_and(m == 1, k == 2))
        def _():
            forward(last)

        y_copy(order(k)).start()

    def back_core(p, q):
        return remote(part.at[p, 1 - c, q], sib.at[p, q], sc_s.at[p, q], sc_r.at[p, q], dev(z, y, 1 - c))

    def back_y(p, q):
        return remote(
            part.at[p, c, q, theirs, :], ybuf.at[p, q], sy_s.at[p, q], sy_r.at[p, q], dev(z, 1 - y, c)
        )

    def back_z(p, q):
        up = p > z
        slot = jnp.where(p == z + 1, PLANES, p)
        return remote(
            part.at[p, c, q, mine, :], zbuf.at[slot, q], sz_s.at[p, q], sz_r.at[slot, q],
            dev(jnp.where(up, z + 1, z - 1), y, c),
        )

    def z_arrival(slot, q):
        ref = zbuf.at[slot, q]
        return remote(ref, ref, sz_s.at[0, q], sz_r.at[slot, q], dev(z, 1 - y, c))

    def down_project(p, q, share):
        cols = pl.ds(pl.multiple_of(q * width, width), width)
        piece = jnp.dot(hidden[...], wd[:, cols], preferred_element_type=jnp.float32)
        piece = (piece * share).astype(jnp.bfloat16)
        part[p, 0, q] = piece[: 2 * n]
        part[p, 1, q] = piece[2 * n :]
        back_core(p, q).start()

    def add_core(p, q):
        back_core(p, q).wait_recv()
        total = part[p, c, q].astype(jnp.float32) + sib[p, q].astype(jnp.float32)
        part[p, c, q] = total.astype(jnp.bfloat16)
        back_y(p, q).start()

    def add_rest(p):
        def body(q, _):
            back_y(p, q).wait_recv()
            acc[...] = part[p, c, q, mine, :].astype(jnp.float32) + ybuf[p, q].astype(jnp.float32)

            def take(slot):
                z_arrival(slot, q).wait_recv()
                acc[...] += zbuf[slot, q].astype(jnp.float32)

            @pl.when(jnp.logical_or(jnp.logical_and(p > z, z > 0), jnp.logical_and(p <= z, z < top)))
            def _():
                take(p)

            @pl.when(jnp.logical_and(p == z, z > 0))
            def _():
                take(PLANES)

            @pl.when(p == z)
            def _():
                out[:, pl.ds(pl.multiple_of(q * width, width), width)] = acc[...].astype(jnp.bfloat16)

            @pl.when(p != z)
            def _():
                part[p, c, q, mine, :] = acc[...].astype(jnp.bfloat16)
                back_z(p, q).start()

            return 0

        lax.fori_loop(0, TILES, body, 0)

    forward(z)
    y_copy(z).start()

    def stage(k, _):
        p = order(k)
        y_arrival(p).wait_recv()
        core_copy(p).start()

        @pl.when(k < top)
        def _():
            advance(k + 1)

        @pl.when(jnp.logical_and(m == 0, k >= 2))
        def _():
            add_rest(order(k - 1))

        core_arrival(p).wait_recv()

        @pl.when(k == 0)
        def _():
            loads[0].wait()
            loads[1].wait()

        table = rows[p, :, :, features:].reshape(4 * n, LANES).astype(jnp.float32)
        lane = lax.broadcasted_iota(jnp.int32, (4 * n, LANES), 1)
        chosen = jnp.logical_or(lane == me, lane == me + LANES // 2)
        share = jnp.sum(jnp.where(chosen, table, 0.0), axis=1, keepdims=True)

        def up_project(j, _):
            cols = pl.ds(pl.multiple_of(j * step_cols, step_cols), step_cols)
            x = rows[p, :, :, :features].reshape(4 * n, features)
            gate = jnp.dot(x, wg[:, cols], preferred_element_type=jnp.float32)
            up = jnp.dot(x, wu[:, cols], preferred_element_type=jnp.float32)
            hidden[:, cols] = (gate / (1.0 + jnp.exp(-gate)) * up).astype(jnp.bfloat16)
            return 0

        lax.fori_loop(0, hid // step_cols, up_project, 0)

        @pl.when(k == 0)
        def _():
            loads[2].wait()

        def down(q, _):
            down_project(p, q, share)

            @pl.when(q > 0)
            def _():
                add_core(p, q - 1)

            return 0

        lax.fori_loop(0, TILES, down, 0)
        add_core(p, TILES - 1)
        return 0

    lax.fori_loop(0, PLANES, stage, 0)

    add_rest(last)

    @pl.when(m == 1)
    def _():
        add_rest(third)
        add_rest(second)

    add_rest(z)

    def settle(p, _):
        @pl.when(goes_up(p))
        def _():
            up_copy(p).wait_send()

        @pl.when(goes_down(p))
        def _():
            down_copy(p).wait_send()

        y_copy(p).wait_send()
        core_copy(p).wait_send()

        def tiles(q, _):
            back_core(p, q).wait_send()
            back_y(p, q).wait_send()

            @pl.when(p != z)
            def _():
                back_z(p, q).wait_send()

            return 0

        lax.fori_loop(0, TILES, tiles, 0)
        return 0

    lax.fori_loop(0, PLANES, settle, 0)


def meshed(tokens, expert_ids, gate_scores, w_gate, w_up, w_down):
    n, features = tokens.shape
    hid = w_gate.shape[1]
    width = features // TILES
    experts = lax.axis_size("node")
    table = routing_table(expert_ids, gate_scores, experts)
    high = table.astype(jnp.bfloat16)
    low = (table - high.astype(jnp.float32)).astype(jnp.bfloat16)
    gap = jnp.zeros((n, LANES // 2 - experts), jnp.bfloat16)
    tok = jnp.concatenate([tokens, high, gap, low, gap], axis=1)
    bf = jnp.bfloat16
    dma = pltpu.SemaphoreType.DMA
    return pl.pallas_call(
        kernel,
        out_shape=jax.ShapeDtypeStruct((n, features), bf),
        in_specs=[pl.BlockSpec(memory_space=pltpu.VMEM)] + [pl.BlockSpec(memory_space=pl.ANY)] * 3,
        out_specs=pl.BlockSpec(memory_space=pltpu.VMEM),
        scratch_shapes=[
            pltpu.VMEM((features, hid), bf),
            pltpu.VMEM((features, hid), bf),
            pltpu.VMEM((hid, features), bf),
            pltpu.VMEM((PLANES, 2, 2 * n, features + LANES), bf),
            pltpu.VMEM((4 * n, hid), bf),
            pltpu.VMEM((PLANES, 2, TILES, 2 * n, width), bf),
            pltpu.VMEM((PLANES, TILES, 2 * n, width), bf),
            pltpu.VMEM((PLANES, TILES, n, width), bf),
            pltpu.VMEM((PLANES + 1, TILES, n, width), bf),
            pltpu.VMEM((n, width), jnp.float32),
            dma((3,)),
            dma((PLANES, 2)), dma((PLANES,)),
            dma((PLANES,)), dma((PLANES,)),
            dma((PLANES,)), dma((PLANES,)),
            dma((PLANES, TILES)), dma((PLANES, TILES)),
            dma((PLANES, TILES)), dma((PLANES, TILES)),
            dma((PLANES, TILES)), dma((PLANES + 1, TILES)),
        ],
        compiler_params=pltpu.CompilerParams(
            collective_id=0, has_side_effects=True, vmem_limit_bytes=62 * 1024 * 1024
        ),
        cost_estimate=pl.CostEstimate(
            flops=6 * 16 * n * features * hid, bytes_accessed=6 * features * hid, transcendentals=16 * n * hid
        ),
    )(tok, w_gate, w_up, w_down)


def gathered(tokens, expert_ids, gate_scores, w_gate, w_up, w_down):
    node_count = lax.axis_size("node")
    experts = max(16, node_count // 2)
    slices = node_count // experts
    table = routing_table(expert_ids, gate_scores, experts)
    all_table = lax.all_gather(table, "node", axis=0, tiled=True)
    share = lax.dynamic_slice_in_dim(all_table, lax.axis_index("node") // slices, 1, 1)
    rows = lax.all_gather(tokens, "node", axis=0, tiled=True)
    gate_part = jnp.dot(rows, w_gate, preferred_element_type=jnp.float32)
    up_part = jnp.dot(rows, w_up, preferred_element_type=jnp.float32)
    hidden = (jax.nn.silu(gate_part) * up_part).astype(jnp.bfloat16)
    piece = jnp.dot(hidden, w_down, preferred_element_type=jnp.float32)
    part = piece * share
    return lax.psum_scatter(part, "node", scatter_dimension=0, tiled=True).astype(jnp.bfloat16)


def solution(mesh):
    return jax.shard_map(
        meshed if mesh.shape["node"] == 16 else gathered,
        mesh=mesh,
        in_specs=(
            P(("group", "node"), None),
            P(("group", "node"), None),
            P(("group", "node"), None),
            P(None, "node"),
            P(None, "node"),
            P("node", None),
        ),
        out_specs=P(("group", "node"), None),
        check_vma=False,
    )
```

```python
import jax
import jax.numpy as jnp
from jax import lax
from jax.experimental import pallas as pl
from jax.experimental.pallas import tpu as pltpu
from jax.sharding import PartitionSpec as P

ROUTE_SCALE = 2.5
PLANES = 4
TILES = 4
LANES = 128
FAR = 1


def routing_table(expert_ids, gate_scores, experts):
    weights = ROUTE_SCALE * gate_scores / jnp.sum(gate_scores, axis=1, keepdims=True)
    marks = expert_ids[:, :, None] == jnp.arange(experts, dtype=jnp.int32)[None, None, :]
    return jnp.sum(jnp.where(marks, weights[:, :, None], 0.0), axis=1)


def kernel(
    tok, wg_hbm, wu_hbm, wd_hbm, out,
    wg, wu, wd, rows, hidden, part, sib, ybuf, zbuf, acc,
    w_sem, gz_s, gz_r, gy_s, gy_r, gb_s, gb_r, gc_s, gc_r, sc_s, sc_r, sy_s, sy_r, sz_s, sz_r,
):
    n = tok.shape[0]
    features = wg_hbm.shape[0]
    hid = wg_hbm.shape[1]
    width = features // TILES
    step_cols = 256
    me = lax.axis_index("node")
    z, y, c = me // 4, (me // 2) % 2, me % 2
    top = PLANES - 1
    mine = pl.ds(pl.multiple_of(y * n, n), n)
    theirs = pl.ds(pl.multiple_of((1 - y) * n, n), n)
    tail = n // 4

    def part_rows(which):
        if which == 0:
            return pl.ds(pl.multiple_of(y * n, n), n - tail)
        at = y if which == 1 else 1 - y
        return pl.ds(pl.multiple_of(at * n + n - tail, tail), tail)

    def dev(zz, yy, cc):
        return {"node": zz * 4 + yy * 2 + cc}

    def remote(src, dst, s, r, target):
        return pltpu.make_async_remote_copy(
            src_ref=src, dst_ref=dst, send_sem=s, recv_sem=r,
            device_id=target, device_id_type=pl.DeviceIdType.MESH,
        )

    loads = [
        pltpu.make_async_copy(a, b, w_sem.at[i])
        for i, (a, b) in enumerate(((wg_hbm, wg), (wu_hbm, wu), (wd_hbm, wd)))
    ]
    for load in loads:
        load.start()
    rows[z, c, mine, :] = tok[...]

    barrier = pltpu.get_barrier_semaphore()

    def greet(target):
        pl.semaphore_signal(barrier, inc=1, device_id=target, device_id_type=pl.DeviceIdType.MESH)

    greet(dev(z, 1 - y, c))
    greet(dev(z, y, 1 - c))

    @pl.when(z > 0)
    def _():
        greet(dev(z - 1, y, c))

    @pl.when(z < top)
    def _():
        greet(dev(z + 1, y, c))

    pl.semaphore_wait(barrier, jnp.where(jnp.logical_or(z == 0, z == top), 3, 4))

    flip = z // 2
    m = z + flip * (top - 2 * z)

    def plane(digit):
        return digit + flip * (top - 2 * digit)

    second, third = plane(1 + m), plane(2 - 2 * m)
    last = plane(3)

    def order(k):
        return jnp.where(k == 0, z, jnp.where(k == 1, second, jnp.where(k == 2, third, last)))

    def z_copy(p, which, up):
        ref = rows.at[p, c, part_rows(which), :]
        way = 0 if up else 1
        return remote(
            ref, ref, gz_s.at[p, way, which], gz_r.at[p, which], dev(z + 1 if up else z - 1, y, c)
        )

    def y_copy(p):
        ref = rows.at[p, c, part_rows(0), :]
        return remote(ref, ref, gy_s.at[p], gy_r.at[p], dev(z, 1 - y, c))

    def y_arrival(p):
        ref = rows.at[p, c, pl.ds(pl.multiple_of((1 - y) * n, n), n - tail), :]
        return remote(ref, ref, gy_s.at[p], gy_r.at[p], dev(z, 1 - y, c))

    def tail_copy(which):
        ref = rows.at[z, c, part_rows(which), :]
        return remote(ref, ref, gb_s.at[0], gb_r.at[0], dev(z, 1 - y, c))

    def core_copy(p):
        ref = rows.at[p, c]
        return remote(ref, ref, gc_s.at[p], gc_r.at[p], dev(z, y, 1 - c))

    def core_arrival(p):
        ref = rows.at[p, 1 - c]
        return remote(ref, ref, gc_s.at[p], gc_r.at[p], dev(z, y, 1 - c))

    def goes_up(p):
        return jnp.logical_and(p <= z, z < top)

    def goes_down(p):
        return jnp.logical_and(p >= z, z > 0)

    def forward(p, which):
        @pl.when(p != z)
        def _():
            ref = rows.at[p, c, part_rows(which), :]
            remote(ref, ref, gz_s.at[p, 0, which], gz_r.at[p, which], dev(z, 1 - y, c)).wait_recv()

        @pl.when(goes_up(p))
        def _():
            z_copy(p, which, True).start()

        @pl.when(goes_down(p))
        def _():
            z_copy(p, which, False).start()

    def forward_all(p):
        for which in range(3):
            forward(p, which)

    def advance(k):
        @pl.when(jnp.logical_and(m == 0, k <= 3))
        def _():
            forward_all(order(k))

        @pl.when(jnp.logical_and(m == 1, k == 1))
        def _():
            forward_all(second)
            forward_all(third)

        @pl.when(jnp.logical_and(m == 1, k == 2))
        def _():
            forward_all(last)

        y_copy(order(k)).start()

    def back_core(p, q):
        return remote(part.at[p, 1 - c, q], sib.at[p, q], sc_s.at[p, q], sc_r.at[p, q], dev(z, y, 1 - c))

    def back_y(p, q):
        return remote(
            part.at[p, c, q, theirs, :], ybuf.at[p, q], sy_s.at[p, q], sy_r.at[p, q], dev(z, 1 - y, c)
        )

    def back_z(p, q):
        up = p > z
        slot = jnp.where(p == z + 1, PLANES, p)
        target = dev(jnp.where(up, z + 1, z - 1), y, c)
        if q < FAR:
            return remote(part.at[p, c, q], zbuf.at[slot, q], sz_s.at[p, q], sz_r.at[slot, q], target)
        return remote(
            part.at[p, c, q, mine, :], zbuf.at[slot, q, pl.ds(0, n), :],
            sz_s.at[p, q], sz_r.at[slot, q], target,
        )

    def z_arrival(slot, q):
        ref = zbuf.at[slot, q] if q < FAR else zbuf.at[slot, q, pl.ds(0, n), :]
        return remote(ref, ref, sz_s.at[0, q], sz_r.at[slot, q], dev(z, 1 - y, c))

    def down_project(p, q, share):
        cols = pl.ds(pl.multiple_of(q * width, width), width)
        piece = jnp.dot(hidden[...], wd[:, cols], preferred_element_type=jnp.float32)
        piece = (piece * share).astype(jnp.bfloat16)
        part[p, 0, q] = piece[: 2 * n]
        part[p, 1, q] = piece[2 * n :]
        back_core(p, q).start()

    def add_core(p, q):
        back_core(p, q).wait_recv()
        total = part[p, c, q].astype(jnp.float32) + sib[p, q].astype(jnp.float32)
        part[p, c, q] = total.astype(jnp.bfloat16)

        @pl.when(q >= FAR)
        def _():
            back_y(p, q).start()

    def add_rest(p):
        for q in range(TILES):
            far = q < FAR
            span = 2 * n if far else n
            here = part.at[p, c, q] if far else part.at[p, c, q, mine, :]
            total = acc.at[pl.ds(0, span), :]
            if far:
                total[...] = here[...].astype(jnp.float32)
            else:
                back_y(p, q).wait_recv()
                total[...] = here[...].astype(jnp.float32) + ybuf[p, q].astype(jnp.float32)

            def take(slot, q=q, span=span, total=total):
                z_arrival(slot, q).wait_recv()
                total[...] += zbuf[slot, q, pl.ds(0, span), :].astype(jnp.float32)

            @pl.when(jnp.logical_or(jnp.logical_and(p > z, z > 0), jnp.logical_and(p <= z, z < top)))
            def _():
                take(p)

            @pl.when(jnp.logical_and(p == z, z > 0))
            def _():
                take(PLANES)

            if far:
                here[...] = total[...].astype(jnp.bfloat16)

                @pl.when(p == z)
                def _():
                    back_y(p, q).start()
            else:
                @pl.when(p == z)
                def _():
                    out[:, q * width : (q + 1) * width] = total[...].astype(jnp.bfloat16)

                @pl.when(p != z)
                def _():
                    here[...] = total[...].astype(jnp.bfloat16)

            @pl.when(p != z)
            def _():
                back_z(p, q).start()

    tail_copy(1).start()
    forward(z, 0)
    forward(z, 1)
    y_copy(z).start()
    tail_copy(2).wait_recv()
    forward(z, 2)

    def stage(k, _):
        p = order(k)
        y_arrival(p).wait_recv()
        core_copy(p).start()

        @pl.when(k < top)
        def _():
            advance(k + 1)

        @pl.when(jnp.logical_and(m == 0, k >= 2))
        def _():
            add_rest(order(k - 1))

        core_arrival(p).wait_recv()

        @pl.when(k == 0)
        def _():
            loads[0].wait()
            loads[1].wait()

        table = rows[p, :, :, features:].reshape(4 * n, LANES).astype(jnp.float32)
        lane = lax.broadcasted_iota(jnp.int32, (4 * n, LANES), 1)
        chosen = jnp.logical_or(lane == me, lane == me + LANES // 2)
        share = jnp.sum(jnp.where(chosen, table, 0.0), axis=1, keepdims=True)

        def up_project(j, _):
            cols = pl.ds(pl.multiple_of(j * step_cols, step_cols), step_cols)
            x = rows[p, :, :, :features].reshape(4 * n, features)
            gate = jnp.dot(x, wg[:, cols], preferred_element_type=jnp.float32)
            up = jnp.dot(x, wu[:, cols], preferred_element_type=jnp.float32)
            hidden[:, cols] = (gate / (1.0 + jnp.exp(-gate)) * up).astype(jnp.bfloat16)
            return 0

        lax.fori_loop(0, hid // step_cols, up_project, 0)

        @pl.when(k == 0)
        def _():
            loads[2].wait()

        def down(q, _):
            down_project(p, q, share)

            @pl.when(q > 0)
            def _():
                add_core(p, q - 1)

            return 0

        lax.fori_loop(0, TILES, down, 0)
        add_core(p, TILES - 1)
        return 0

    lax.fori_loop(0, PLANES, stage, 0)

    def remaining(i, _):
        @pl.when(jnp.logical_or(m == 1, jnp.logical_or(i == 1, i == 3)))
        def _():
            add_rest(jnp.where(i == 0, second, jnp.where(i == 1, last, jnp.where(i == 2, third, z))))

        return 0

    lax.fori_loop(0, PLANES, remaining, 0)
    for q in range(FAR):
        back_y(z, q).wait_recv()
        total = part[z, c, q, mine, :].astype(jnp.float32) + ybuf[z, q].astype(jnp.float32)
        out[:, q * width : (q + 1) * width] = total.astype(jnp.bfloat16)

    def settle(p, _):
        @pl.when(goes_up(p))
        def _():
            for which in range(3):
                z_copy(p, which, True).wait_send()

        @pl.when(goes_down(p))
        def _():
            for which in range(3):
                z_copy(p, which, False).wait_send()

        y_copy(p).wait_send()
        core_copy(p).wait_send()

        for q in range(TILES):
            back_core(p, q).wait_send()

            @pl.when(jnp.logical_or(q >= FAR, p == z))
            def _():
                back_y(p, q).wait_send()

            @pl.when(p != z)
            def _():
                back_z(p, q).wait_send()

        return 0

    lax.fori_loop(0, PLANES, settle, 0)
    tail_copy(1).wait_send()


def meshed(tokens, expert_ids, gate_scores, w_gate, w_up, w_down):
    n, features = tokens.shape
    hid = w_gate.shape[1]
    width = features // TILES
    experts = lax.axis_size("node")
    table = routing_table(expert_ids, gate_scores, experts)
    high = table.astype(jnp.bfloat16)
    low = (table - high.astype(jnp.float32)).astype(jnp.bfloat16)
    gap = jnp.zeros((n, LANES // 2 - experts), jnp.bfloat16)
    tok = jnp.concatenate([tokens, high, gap, low, gap], axis=1)
    bf = jnp.bfloat16
    dma = pltpu.SemaphoreType.DMA
    return pl.pallas_call(
        kernel,
        out_shape=jax.ShapeDtypeStruct((n, features), bf),
        in_specs=[pl.BlockSpec(memory_space=pltpu.VMEM)] + [pl.BlockSpec(memory_space=pl.ANY)] * 3,
        out_specs=pl.BlockSpec(memory_space=pltpu.VMEM),
        scratch_shapes=[
            pltpu.VMEM((features, hid), bf),
            pltpu.VMEM((features, hid), bf),
            pltpu.VMEM((hid, features), bf),
            pltpu.VMEM((PLANES, 2, 2 * n, features + LANES), bf),
            pltpu.VMEM((4 * n, hid), bf),
            pltpu.VMEM((PLANES, 2, TILES, 2 * n, width), bf),
            pltpu.VMEM((PLANES, TILES, 2 * n, width), bf),
            pltpu.VMEM((PLANES, TILES, n, width), bf),
            pltpu.VMEM((PLANES + 1, TILES, 2 * n, width), bf),
            pltpu.VMEM((2 * n, width), jnp.float32),
            dma((3,)),
            dma((PLANES, 2, 3)), dma((PLANES, 3)),
            dma((PLANES,)), dma((PLANES,)),
            dma((1,)), dma((1,)),
            dma((PLANES,)), dma((PLANES,)),
            dma((PLANES, TILES)), dma((PLANES, TILES)),
            dma((PLANES, TILES)), dma((PLANES, TILES)),
            dma((PLANES, TILES)), dma((PLANES + 1, TILES)),
        ],
        compiler_params=pltpu.CompilerParams(
            collective_id=0, has_side_effects=True, vmem_limit_bytes=62 * 1024 * 1024
        ),
        cost_estimate=pl.CostEstimate(
            flops=6 * 16 * n * features * hid, bytes_accessed=6 * features * hid, transcendentals=16 * n * hid
        ),
    )(tok, w_gate, w_up, w_down)


def gathered(tokens, expert_ids, gate_scores, w_gate, w_up, w_down):
    node_count = lax.axis_size("node")
    experts = max(16, node_count // 2)
    slices = node_count // experts
    table = routing_table(expert_ids, gate_scores, experts)
    all_table = lax.all_gather(table, "node", axis=0, tiled=True)
    share = lax.dynamic_slice_in_dim(all_table, lax.axis_index("node") // slices, 1, 1)
    rows = lax.all_gather(tokens, "node", axis=0, tiled=True)
    gate_part = jnp.dot(rows, w_gate, preferred_element_type=jnp.float32)
    up_part = jnp.dot(rows, w_up, preferred_element_type=jnp.float32)
    hidden = (jax.nn.silu(gate_part) * up_part).astype(jnp.bfloat16)
    piece = jnp.dot(hidden, w_down, preferred_element_type=jnp.float32)
    part = piece * share
    return lax.psum_scatter(part, "node", scatter_dimension=0, tiled=True).astype(jnp.bfloat16)


def solution(mesh):
    return jax.shard_map(
        meshed if mesh.shape["node"] == 16 else gathered,
        mesh=mesh,
        in_specs=(
            P(("group", "node"), None),
            P(("group", "node"), None),
            P(("group", "node"), None),
            P(None, "node"),
            P(None, "node"),
            P("node", None),
        ),
        out_specs=P(("group", "node"), None),
        check_vma=False,
    )
```
